32 devices in a mesh: dp: 8 (over z, x), expert: 4 (over y, core).
Axes of the slice: x: 2, y: 2, z: 4, core: 2. Of those that a mesh axis runs over, the one named last changes fastest.
Arguments:
- grad_out: bfloat16 [4096, 1536], P(('dp', 'expert')), may hold values from -6 to 6
- expert_ids: int32 [4096, 2], P(('dp', 'expert')), may hold values from 0 to 3, all different within a row; in each aligned block of 128 rows (0 to 127, 128 to 255, ...) at most 96 rows name the same one
- gates: float32 [4096, 2], P(('dp', 'expert')), may hold values from 0.1 to 1
- routed_pre: bfloat16 [8, 4, 384, 3072], P('dp', 'expert'), may hold values from -6 to 6
- routed_down: bfloat16 [4, 3072, 1536], P('expert', 'dp'), may hold values from -0.109375 to 0.109375
- shared_pre: bfloat16 [4096, 6144], P('dp', 'expert'), may hold values from -6 to 6
- shared_down: bfloat16 [6144, 1536], P(('expert', 'dp')), may hold values from -0.078125 to 0.078125
Outputs:
- routed_pre_grad: bfloat16 [8, 4, 384, 3072], P('dp', 'expert')
- routed_down_grad: float32 [4, 3072, 1536], P('expert', 'dp')
- shared_pre_grad: bfloat16 [4096, 6144], P('dp', 'expert')
- shared_down_grad: float32 [6144, 1536], P(('expert', 'dp'))
- gate_grad: float32 [4096, 2], P(('dp', 'expert'))
The draws below stay inside these ranges and needn't reach their ends.
Inputs may be any that keep to these rules, and one draw needn't show every extreme that they name: `expert_ids`: each row names two different experts. Among the 128 rows of one device no expert is named more than 96 times, and in every draw some expert is named exactly 96 times by the rows of some device.
All inputs are finite; a program needn't handle non-finite values.
Results may differ from the reference program's by a relative error of at most 0.015.
Values may be sent and summed in bfloat16 or wider, within the bound.
A program may use at most 128 MiB of HBM per device.

```python
import math
import jax
import jax.numpy as jnp
import numpy as np
from jax import lax

D = 1536
H = 3072
HS = 6144
TOK_DEV = 128
EXPERTS = 4
CAP = 96
SLOTS = 384
ROW_TOK = 512
TOKENS = 4096
N_DP = 8
N_EXPERT = 4


def strengthened(array, rng, source, target, parts, factor):
    owner, partner = [(jnp.arange(array.shape[axis_at]) // (array.shape[axis_at] // parts)).reshape([-1 if axis == axis_at else 1 for axis in range(array.ndim)]) for axis_at in (source, target)]
    chosen = jax.random.permutation(rng, parts)[partner]
    strong = (owner == chosen) | (owner == (partner + parts // 2) % parts)
    return jnp.where(strong, factor * array, array)


def steps_of(own_key, shape, shards, least, largest):
    level = 1.0
    for dim, parts in shards:
        draws = jax.random.uniform(jax.random.fold_in(jax.random.fold_in(own_key, 6), dim), (parts,), jnp.float32, least / len(shards), largest / len(shards))
        level = level * jnp.repeat(jnp.exp(draws), shape[dim] // parts).reshape((-1,) + (1,) * (len(shape) - 1 - dim))
    return level


def deal_out(stream_key, own, number, rows, count, top, most, skew):
    sequence = jax.random.permutation(stream_key, count)
    heavy_load, usual = shares(count, rows * top, most, skew, True), shares(count, rows * top, most, skew, False)
    places = jnp.arange(count)

    def named(tallies, offset_by):
        used = int((tallies > 0).sum())
        fixed = max(1, used // 4)
        moved = fixed + (places - fixed + offset_by * (used - fixed)) % max(1, count - fixed)
        return jnp.zeros((count,), jnp.int32).at[sequence[jnp.where(places < fixed, places, moved)]].set(jnp.asarray(tallies, jnp.int32))

    tallies = jnp.where(number % 4 == 0, named(heavy_load, number // 4), named(usual, number - number // 4 - 1))
    mixed = jax.random.permutation(jax.random.fold_in(own, 3), count)
    donor, receiver = mixed[0:count // 2 * 2:2], mixed[1:count // 2 * 2:2]
    room = jnp.minimum(tallies[donor] - 1, most - tallies[receiver]) // 2
    room = jnp.where((donor == sequence[0]) | (receiver == sequence[0]) | (tallies[receiver] == 0), 0, jnp.maximum(room, 0))
    moved = jax.random.randint(jax.random.fold_in(own, 4), (count // 2,), 0, 1 << 20) % (room + 1)
    tallies = tallies.at[donor].add(-moved).at[receiver].add(moved)
    members = jnp.searchsorted(jnp.cumsum(tallies), jnp.arange(rows * top), side="right").astype(jnp.int32)
    listing = members.reshape(top, rows).T
    listing = listing[jax.random.permutation(jax.random.fold_in(own, 1), rows)]
    offset_by = jax.random.randint(jax.random.fold_in(own, 2), (rows, 1), 0, top)
    return jnp.take_along_axis(listing, (jnp.arange(top)[None, :] + offset_by) % top, axis=1)


def shares(number_of, total, limit, skew, full):
    weights = [(1 << 20) // math.isqrt(rank ** skew) + 1 for rank in range(1, number_of + 1)]
    largest = limit if full else min(limit, max(-(-total // number_of), total * weights[0] // sum(weights)))
    least = 1 if total - largest >= number_of - 1 else 0
    counts, surplus = [largest] + [least] * (number_of - 1), total - largest - least * (number_of - 1)
    while surplus > 0:
        candidates = [i for i in range(1, number_of) if counts[i] < largest] or [i for i in range(1, number_of) if counts[i] < limit]
        whole, budget = sum([weights[i] for i in candidates]), surplus
        for i in candidates:
            addition = min(limit - counts[i], max(1, budget * weights[i] // whole), surplus)
            counts[i] = counts[i] + addition
            surplus = surplus - addition
    return np.array(counts)


def gaussian(key, extent, deviation, bound, split=(), kind=jnp.bfloat16):
    factor_of = steps_of(key, extent, split, -0.22, 0.18) if split else 1.0
    result = jax.random.normal(key, extent, jnp.float32) * deviation * factor_of
    return jnp.minimum(jnp.maximum(result, -bound), bound).astype(kind)


def gaussian_with(key, dims, scale, limit, pieces, heavy, kind=jnp.bfloat16):
    result = scale * jax.random.normal(key, dims, jnp.float32)
    if pieces:
        result = result * steps_of(key, dims, pieces, -0.22, 0.18)
    return jnp.clip(strengthened(result, jax.random.fold_in(key, 3), *heavy), -limit, limit).astype(kind)


def setup_inputs(seed: int = 0) -> dict:
    key_list = jax.random.split(jax.random.key(seed), 8)
    grad_out = gaussian(key_list[0], (TOKENS, D), 1.0, 6.0, ((0, 32),))
    expert_ids_keys = jax.random.split(jax.random.fold_in(key_list[1], 1), TOKENS // TOK_DEV)
    expert_ids_turns = jax.random.permutation(jax.random.fold_in(key_list[1], 3), TOKENS // TOK_DEV)
    expert_ids = jax.vmap(lambda own, number: deal_out(jax.random.fold_in(key_list[1], 2), own, number, TOK_DEV, EXPERTS, 2, CAP, 2))(expert_ids_keys, expert_ids_turns).reshape((TOKENS, 2))
    gates = jnp.clip(0.1 + 0.9 * jax.random.uniform(key_list[2], (TOKENS, 2), jnp.float32) ** steps_of(key_list[2], (TOKENS, 2), ((0, 32),), -0.2, 0.2), 0.1, 1.0)
    routed_pre = gaussian_with(key_list[3], (N_DP, EXPERTS, SLOTS, H), 1.0, 6.0, ((0, 8), (1, 4)), (0, 3, 8, 2.0))
    routed_down = gaussian(key_list[4], (EXPERTS, H, D), H ** -0.5, 0.109375, ((0, 4), (1, 8)))
    shared_pre = gaussian_with(key_list[5], (TOKENS, HS), 1.0, 6.0, ((0, 8), (1, 4)), (0, 1, 8, 2.0))
    shared_down = gaussian(key_list[6], (HS, D), HS ** -0.5, 0.078125, ((0, 32),))
    return {"grad_out": grad_out, "expert_ids": expert_ids, "gates": gates, "routed_pre": routed_pre, "routed_down": routed_down, "shared_pre": shared_pre, "shared_down": shared_down}


SQRT_TWO_PI = 0.7978845608028654


def gelu_pair(inputs):
    cubic = inputs * inputs * inputs
    tangent = jnp.tanh(SQRT_TWO_PI * (inputs + 0.044715 * cubic))
    value = 0.5 * inputs * (1.0 + tangent)
    slope = 0.5 * (1.0 + tangent) + 0.5 * inputs * (1.0 - tangent * tangent) * SQRT_TWO_PI * (1.0 + 3.0 * 0.044715 * inputs * inputs)
    return value, slope


def slot_ranks(flat_ids, experts):
    labels = jnp.arange(experts, dtype=jnp.int32)
    onehot = (flat_ids[:, :, None] == labels[None, None, :]).astype(jnp.int32)
    before = jnp.cumsum(onehot, axis=1) - onehot
    return jnp.sum(before * onehot, axis=2).astype(jnp.int32)


def reference(grad_out, expert_ids, gates, routed_pre, routed_down, shared_pre, shared_down):
    blocks = TOKENS // TOK_DEV
    rank = slot_ranks(expert_ids.reshape(blocks, TOK_DEV * 2), EXPERTS)
    source = (jnp.arange(blocks, dtype=jnp.int32) % N_EXPERT)[:, None]
    slot = (source * CAP + rank).astype(jnp.int32).reshape(N_DP, ROW_TOK * 2)
    ids = expert_ids.reshape(N_DP, ROW_TOK * 2)
    gate_b = gates.astype(jnp.bfloat16).reshape(N_DP, ROW_TOK * 2)
    rows = grad_out.reshape(N_DP, ROW_TOK, D)
    shared_rows = shared_pre.reshape(N_DP, ROW_TOK, HS)
    routed_weight = routed_down.astype(jnp.float32)

    def step(totals, inputs):
        routed_total, shared_total = totals
        ids_d, slot_d, gate_d, rows_d, pre_d, spre_d = inputs
        twice = jnp.repeat(rows_d, 2, axis=0)
        routed_in = jnp.zeros((EXPERTS, SLOTS, D), jnp.bfloat16).at[ids_d, slot_d].set(twice)
        routed_gate = jnp.zeros((EXPERTS, SLOTS), jnp.bfloat16).at[ids_d, slot_d].set(gate_d)
        value, slope = gelu_pair(pre_d.astype(jnp.float32))
        hidden_b = value.astype(jnp.bfloat16)
        raw = jnp.einsum("esd,ehd->esh", routed_in.astype(jnp.float32), routed_weight)
        gate_col = routed_gate.astype(jnp.float32)[:, :, None]
        pre_grad = (gate_col * raw * slope).astype(jnp.bfloat16)
        score = jnp.sum(value * raw, axis=2)
        scaled = (gate_col * routed_in.astype(jnp.float32)).astype(jnp.bfloat16)
        term = jnp.einsum("esh,esd->ehd", hidden_b.astype(jnp.float32), scaled.astype(jnp.float32))
        term_b = lax.optimization_barrier(term.astype(jnp.bfloat16))
        routed_total = routed_total + term_b.astype(jnp.float32)
        gate_grad_d = score[ids_d, slot_d]
        svalue, sslope = gelu_pair(spre_d.astype(jnp.float32))
        shared_b = svalue.astype(jnp.bfloat16)
        raw_shared = jnp.dot(rows_d, shared_down.T, preferred_element_type=jnp.float32)
        spre_grad = (raw_shared * sslope).astype(jnp.bfloat16)
        sterm = jnp.dot(shared_b.T, rows_d, preferred_element_type=jnp.float32)
        sterm_b = lax.optimization_barrier(sterm.astype(jnp.bfloat16))
        shared_total = shared_total + sterm_b.astype(jnp.float32)
        return (routed_total, shared_total), (pre_grad, gate_grad_d, spre_grad)

    start = (jnp.zeros((EXPERTS, H, D), jnp.float32), jnp.zeros((HS, D), jnp.float32))
    totals, outputs = lax.scan(step, start, (ids, slot, gate_b, rows, routed_pre, shared_rows))
    routed_total, shared_total = totals
    pre_grads, gate_grads, spre_grads = outputs
    return pre_grads, routed_total, spre_grads.reshape(TOKENS, HS), shared_total, gate_grads.reshape(TOKENS, 2)
```

```python
import functools

import jax
import jax.numpy as jnp
from jax import lax
from jax.experimental import pallas as pl
from jax.experimental.pallas import tpu as pltpu
from jax.sharding import PartitionSpec as P

SQRT_TWO_PI = 0.7978845608028654


def gelu_pair(inputs):
    cubic = inputs * inputs * inputs
    tangent = jnp.tanh(SQRT_TWO_PI * (inputs + 0.044715 * cubic))
    value = 0.5 * inputs * (1.0 + tangent)
    slope = 0.5 * (1.0 + tangent) + 0.5 * inputs * (1.0 - tangent * tangent) * SQRT_TWO_PI * (
        1.0 + 3.0 * 0.044715 * inputs * inputs
    )
    return (value, slope)


def slot_ranks(flat_ids, experts):
    labels = jnp.arange(experts, dtype=jnp.int32)
    onehot = (flat_ids[:, :, None] == labels[None, None, :]).astype(jnp.int32)
    before = jnp.cumsum(onehot, axis=1) - onehot
    return jnp.sum(before * onehot, axis=2)


def body(grad_out, expert_ids, gates, routed_pre, routed_down, shared_pre, shared_down):
    n_exp = lax.axis_size("expert")
    tok = grad_out.shape[0]
    width = grad_out.shape[1]
    slots = routed_pre.shape[2]
    cap = slots // n_exp
    owner = lax.axis_index("expert")
    gate_b = gates.astype(jnp.bfloat16)
    whole_down, whole_shared = (
        lax.all_gather(routed_down, "dp", axis=1, tiled=True),
        lax.all_gather(shared_down, "dp", axis=0, tiled=True),
    )
    own_rank = slot_ranks(expert_ids.reshape(1, tok * 2), n_exp).reshape(tok, 2)
    group_rows, group_gate = (
        lax.all_gather(grad_out, "expert", axis=0, tiled=True),
        lax.all_gather(gate_b, "expert", axis=0, tiled=True),
    )
    group_ids = lax.all_gather(expert_ids, "expert", axis=0, tiled=True)
    group_rank = slot_ranks(group_ids.reshape(n_exp, tok * 2), n_exp).reshape(n_exp * tok, 2)
    source = jnp.arange(n_exp * tok, dtype=jnp.int32) // tok
    target = jnp.where(group_ids == owner, source[:, None] * cap + group_rank, slots)
    recv_rows = jnp.zeros((slots + 1, width), jnp.bfloat16)
    recv_rows = recv_rows.at[target[:, 0]].set(group_rows).at[target[:, 1]].set(group_rows)[:slots]
    recv_gate = jnp.zeros((slots + 1,), jnp.bfloat16).at[target].set(group_gate)[:slots]
    value, slope = gelu_pair(routed_pre[0, 0].astype(jnp.float32))
    hidden_b = value.astype(jnp.bfloat16)
    raw = lax.dot_general(
        recv_rows, whole_down[0], (((1,), (1,)), ((), ())), preferred_element_type=jnp.float32
    )
    gate_col = recv_gate.astype(jnp.float32)[:, None]
    routed_pre_grad = (gate_col * raw * slope).astype(jnp.bfloat16).reshape(routed_pre.shape)
    slot_score = jnp.sum(value * raw, axis=1)
    scaled = (gate_col * recv_rows.astype(jnp.float32)).astype(jnp.bfloat16)
    routed_term = lax.dot_general(
        hidden_b, scaled, (((0,), (0,)), ((), ())), preferred_element_type=jnp.float32
    )
    returned = lax.all_to_all(
        slot_score.reshape(n_exp, cap), "expert", split_axis=0, concat_axis=0, tiled=True
    )
    gate_grad = returned[expert_ids, own_rank]
    svalue, sslope = gelu_pair(shared_pre.astype(jnp.float32))
    shared_b = svalue.astype(jnp.bfloat16)
    raw_shared = lax.dot_general(
        group_rows, whole_shared, (((1,), (1,)), ((), ())), preferred_element_type=jnp.float32
    )
    shared_pre_grad = (raw_shared * sslope).astype(jnp.bfloat16)
    shared_term = lax.dot_general(
        shared_b, group_rows, (((0,), (0,)), ((), ())), preferred_element_type=jnp.float32
    )
    routed_sum, shared_sum = (
        lax.psum_scatter(
            routed_term.astype(jnp.bfloat16), "dp", scatter_dimension=0, tiled=True
        ).astype(jnp.float32),
        lax.psum_scatter(
            shared_term.astype(jnp.bfloat16), "dp", scatter_dimension=0, tiled=True
        ).astype(jnp.float32),
    )
    return (
        routed_pre_grad,
        routed_sum.reshape(1, routed_sum.shape[0], width),
        shared_pre_grad,
        shared_sum,
        gate_grad,
    )


def flip(value, mask, bits):
    out = 0
    for bit in range(bits):
        has = lax.rem(value // (1 << bit), 2)
        out = out + ((1 - has) if (mask >> bit) & 1 else has) * (1 << bit)
    return out


def flip_by(value, mask, bits):
    out = 0
    for bit in range(bits):
        a, b = lax.rem(value // (1 << bit), 2), lax.rem(mask // (1 << bit), 2)
        out = out + (a + b - 2 * a * b) * (1 << bit)
    return out


def token_kernel(
    dp_bits, exp_bits, cap,
    grad, meta, pre_r, pre_s, down_r, down_s,
    out_r, out_s, grad_r, grad_s, gate_out,
    rows, metas, in_r, in_s, stage_r, stage_s, routed, scaled, gate_part, gate_recv, gate_sum, gate_last,
    ag_send, ag_recv, m1_send, m1_recv, m2_send, m2_recv,
    inr_send, inr_recv, ins_send, ins_recv, outr_send, outr_recv, outs_send, outs_recv,
    g1_send, g1_recv, g2_send, g2_recv, local,
):
    n_dp, n_exp = 1 << dp_bits, 1 << exp_bits
    d, e = lax.axis_index("dp"), lax.axis_index("expert")
    own = d * n_exp + e
    bits = dp_bits + exp_bits
    tok = grad.shape[0]
    hid_r, hid_s = down_r.shape[0], down_s.shape[0]
    group = n_exp * tok

    def dp_peer(mask):
        return {"dp": flip(d, mask, dp_bits), "expert": e}

    def exp_peer(mask):
        return {"dp": d, "expert": flip(e, mask, exp_bits)}

    def peer(bit):
        return exp_peer(1 << bit) if bit < exp_bits else dp_peer(1 << (bit - exp_bits))

    def remote(source, target, send, recv, device):
        return pltpu.make_async_remote_copy(
            src_ref=source, dst_ref=target, send_sem=send, recv_sem=recv,
            device_id=device, device_id_type=pl.DeviceIdType.MESH,
        )

    barrier = pltpu.get_barrier_semaphore()
    for mask in range(1, n_dp):
        pl.semaphore_signal(barrier, inc=1, device_id=dp_peer(mask), device_id_type=pl.DeviceIdType.MESH)
    for mask in range(1, n_exp):
        pl.semaphore_signal(barrier, inc=1, device_id=exp_peer(mask), device_id_type=pl.DeviceIdType.MESH)

    def rows_of(mask):
        at = pl.multiple_of(flip(own, mask, bits) * tok, tok)
        return rows.at[pl.ds(at, tok), :]

    rows[pl.ds(pl.multiple_of(own * tok, tok), tok), :] = grad[...]
    metas[d, e] = meta[...]
    own_r = pltpu.make_async_copy(
        pre_r.at[:, pl.ds(pl.multiple_of(d * hid_r, hid_r), hid_r)], in_r.at[0], local.at[0]
    )
    own_s = pltpu.make_async_copy(
        pre_s.at[pl.ds(pl.multiple_of(d * hid_s, hid_s), hid_s), :], in_s.at[0], local.at[1]
    )
    own_r.start()
    own_s.start()
    pl.semaphore_wait(barrier, n_dp + n_exp - 2)

    def hop(mask, bit):
        got = mask | (1 << bit)
        return remote(rows_of(mask), rows_of(mask), ag_send.at[got], ag_recv.at[got], peer(bit))

    def arrived(mask):
        return remote(rows_of(mask), rows_of(mask), ag_send.at[mask], ag_recv.at[mask], peer(0))

    order = list(range(bits))[::-1]
    meta_first = [
        remote(metas.at[d, e], metas.at[d, e], m1_send.at[mask], m1_recv.at[mask], exp_peer(mask))
        for mask in range(1, n_exp)
    ]
    for copy in meta_first:
        copy.start()
    for bit in order:
        hop(0, bit).start()
    for mask in range(n_dp - 1, 0, -1):
        to = flip(d, mask, dp_bits)
        remote(
            pre_r.at[:, pl.ds(pl.multiple_of(to * hid_r, hid_r), hid_r)],
            in_r.at[mask], inr_send.at[mask], inr_recv.at[mask], dp_peer(mask),
        ).start()
        remote(
            pre_s.at[pl.ds(pl.multiple_of(to * hid_s, hid_s), hid_s), :],
            in_s.at[mask], ins_send.at[mask], ins_recv.at[mask], dp_peer(mask),
        ).start()
    for mask in range(1, n_exp):
        came = metas.at[d, flip(e, mask, exp_bits)]
        remote(came, came, m1_send.at[mask], m1_recv.at[mask], exp_peer(mask)).wait_recv()
    for mask in range(1, n_dp):
        remote(metas.at[d], metas.at[d], m2_send.at[mask], m2_recv.at[mask], dp_peer(mask)).start()

    grad_r[...] = jnp.zeros_like(grad_r)
    grad_s[...] = jnp.zeros_like(grad_s)
    gate_part[...] = jnp.zeros_like(gate_part)

    held = [0]
    for place, bit in enumerate(order):
        fresh = [mask | (1 << bit) for mask in held]
        for mask in fresh:
            arrived(mask).wait_recv()
            for later in order[place + 1:]:
                hop(mask, later).start()
        held = held + fresh
    for mask in range(1, n_dp):
        came = metas.at[flip(d, mask, dp_bits)]
        remote(came, came, m2_send.at[mask], m2_recv.at[mask], dp_peer(mask)).wait_recv()
    own_r.wait()
    own_s.wait()

    columns = pl.ds(pl.multiple_of(d * hid_r, hid_r), hid_r)
    lines = pl.ds(pl.multiple_of(d * hid_s, hid_s), hid_s)

    @pl.loop(0, n_dp)
    def _(turn):
        mask = n_dp - 1 - turn
        p = flip_by(d, mask, dp_bits)
        target = {"dp": p, "expert": e}

        @pl.when(mask > 0)
        def _():
            remote(in_r.at[mask], in_r.at[mask], inr_send.at[mask], inr_recv.at[mask], target).wait_recv()
            remote(in_s.at[mask], in_s.at[mask], ins_send.at[mask], ins_recv.at[mask], target).wait_recv()

        group_rows = rows[pl.ds(pl.multiple_of(p * group, group), group), :]
        raw_s = lax.dot_general(
            down_s[...], group_rows, (((1,), (1,)), ((), ())), preferred_element_type=jnp.float32
        )
        value_s, slope_s = gelu_pair(in_s[mask].astype(jnp.float32))
        stage_s[mask] = (raw_s * slope_s).astype(jnp.bfloat16)

        gate_cols = []
        picks = []
        line = lax.broadcasted_iota(jnp.int32, (cap, tok), 0).astype(jnp.float32)
        expert = e.astype(jnp.float32)
        for s in range(n_exp):
            info = metas[p, s]
            pick0 = (info[0:1] == expert) & (info[2:3] == line)
            pick1 = (info[1:2] == expert) & (info[3:4] == line)
            gate = info[4:6].astype(jnp.bfloat16).astype(jnp.float32)
            weight = jnp.where(pick0, gate[0:1], 0.0) + jnp.where(pick1, gate[1:2], 0.0)
            chosen = (jnp.where(pick0, 1.0, 0.0) + jnp.where(pick1, 1.0, 0.0)).astype(jnp.bfloat16)
            block = lax.dot_general(
                chosen, group_rows[s * tok:(s + 1) * tok], (((1,), (0,)), ((), ())),
                preferred_element_type=jnp.float32,
            )
            gate_col = jnp.sum(weight, axis=1, keepdims=True)
            routed[s * cap:(s + 1) * cap, :] = block.astype(jnp.bfloat16)
            scaled[s * cap:(s + 1) * cap, :] = (gate_col * block).astype(jnp.bfloat16)
            gate_cols.append(gate_col)
            picks.append((pick0, pick1))
        raw = lax.dot_general(
            routed[...], down_r[...], (((1,), (1,)), ((), ())), preferred_element_type=jnp.float32
        )
        value, slope = gelu_pair(in_r[mask].astype(jnp.float32))
        stage_r[mask] = (jnp.concatenate(gate_cols, axis=0) * raw * slope).astype(jnp.bfloat16)
        score = jnp.sum(value * raw, axis=1, keepdims=True)
        for s in range(n_exp):
            part = score[s * cap:(s + 1) * cap]
            for k in range(2):
                gate_part[mask, s, k:k + 1, :] = jnp.sum(
                    jnp.where(picks[s][k], part, 0.0), axis=0, keepdims=True
                )

        @pl.when(mask > 0)
        def _():
            remote(stage_r.at[mask], out_r.at[:, columns], outr_send.at[mask], outr_recv.at[mask], target).start()
            remote(stage_s.at[mask], out_s.at[lines, :], outs_send.at[mask], outs_recv.at[mask], target).start()
            remote(gate_part.at[mask], gate_recv.at[mask], g1_send.at[mask], g1_recv.at[mask], target).start()

        grad_s[...] += lax.dot_general(
            value_s.astype(jnp.bfloat16), group_rows, (((1,), (0,)), ((), ())), preferred_element_type=jnp.float32
        )
        grad_r[...] += lax.dot_general(
            value.astype(jnp.bfloat16), scaled[...], (((0,), (0,)), ((), ())), preferred_element_type=jnp.float32
        )

    last_r = pltpu.make_async_copy(stage_r.at[0], out_r.at[:, columns], local.at[2])
    last_s = pltpu.make_async_copy(stage_s.at[0], out_s.at[lines, :], local.at[3])
    last_r.start()
    last_s.start()

    total = gate_part[0]
    for mask in range(1, n_dp):
        remote(
            gate_recv.at[mask], gate_recv.at[mask], g1_send.at[mask], g1_recv.at[mask], dp_peer(mask)
        ).wait_recv()
        total = total + gate_recv[mask]
    gate_sum[...] = total
    for mask in range(1, n_exp):
        remote(
            gate_sum.at[flip(e, mask, exp_bits)], gate_last.at[mask], g2_send.at[mask], g2_recv.at[mask], exp_peer(mask)
        ).start()
    final = gate_sum[e]
    for mask in range(1, n_exp):
        remote(
            gate_last.at[mask], gate_last.at[mask], g2_send.at[mask], g2_recv.at[mask], exp_peer(mask)
        ).wait_recv()
        final = final + gate_last[mask]
    gate_out[...] = final

    for mask in range(1, n_dp):
        origin = flip(d, mask, dp_bits)
        from_r = out_r.at[:, pl.ds(pl.multiple_of(origin * hid_r, hid_r), hid_r)]
        from_s = out_s.at[pl.ds(pl.multiple_of(origin * hid_s, hid_s), hid_s), :]
        remote(stage_r.at[mask], from_r, outr_send.at[mask], outr_recv.at[mask], dp_peer(mask)).wait()
        remote(stage_s.at[mask], from_s, outs_send.at[mask], outs_recv.at[mask], dp_peer(mask)).wait()
        remote(in_r.at[mask], in_r.at[mask], inr_send.at[mask], inr_recv.at[mask], dp_peer(mask)).wait_send()
        remote(in_s.at[mask], in_s.at[mask], ins_send.at[mask], ins_recv.at[mask], dp_peer(mask)).wait_send()
        remote(metas.at[d], metas.at[d], m2_send.at[mask], m2_recv.at[mask], dp_peer(mask)).wait_send()
        remote(
            gate_part.at[mask], gate_recv.at[mask], g1_send.at[mask], g1_recv.at[mask], dp_peer(mask)
        ).wait_send()
    for mask in range(1, n_exp):
        remote(metas.at[d, e], metas.at[d, e], m1_send.at[mask], m1_recv.at[mask], exp_peer(mask)).wait_send()
        remote(
            gate_sum.at[flip(e, mask, exp_bits)], gate_last.at[mask], g2_send.at[mask], g2_recv.at[mask], exp_peer(mask)
        ).wait_send()
    for mask in range(1, n_dp * n_exp):
        arrived(mask).wait_send()
    last_r.wait()
    last_s.wait()


def token_body(grad_out, expert_ids, gates, routed_pre, routed_down, shared_pre, shared_down):
    n_dp, n_exp = lax.axis_size("dp"), lax.axis_size("expert")
    dp_bits, exp_bits = n_dp.bit_length() - 1, n_exp.bit_length() - 1
    tok, width = grad_out.shape
    slots, hidden = routed_pre.shape[2:]
    cap = slots // n_exp
    hid_r, hid_s = routed_down.shape[1], shared_down.shape[0]
    group, shared_hidden = shared_pre.shape
    flat = expert_ids.reshape(tok * 2)
    place = jnp.arange(tok * 2, dtype=jnp.int32)
    rank = jnp.sum(
        ((flat[None, :] == flat[:, None]) & (place[None, :] < place[:, None])).astype(jnp.float32), axis=1
    ).reshape(tok, 2)
    meta = jnp.concatenate(
        [expert_ids.astype(jnp.float32).T, rank.T, gates.T, jnp.zeros((2, tok), jnp.float32)], axis=0
    )
    any_spec, vmem = pl.BlockSpec(memory_space=pl.ANY), pl.BlockSpec(memory_space=pltpu.VMEM)
    bf, f32, dma = jnp.bfloat16, jnp.float32, pltpu.SemaphoreType.DMA
    every = n_dp * n_exp
    flops = 4 * n_dp * width * (slots * hid_r + group * hid_s)
    out_r, out_s, grad_r, grad_s, gate = pl.pallas_call(
        functools.partial(token_kernel, dp_bits, exp_bits, cap),
        out_shape=[
            jax.ShapeDtypeStruct((slots, hidden), bf),
            jax.ShapeDtypeStruct((shared_hidden, group), bf),
            jax.ShapeDtypeStruct((hid_r, width), f32),
            jax.ShapeDtypeStruct((hid_s, width), f32),
            jax.ShapeDtypeStruct((8, tok), f32),
        ],
        in_specs=[vmem, vmem, any_spec, any_spec, vmem, vmem],
        out_specs=[any_spec, any_spec, vmem, vmem, vmem],
        scratch_shapes=[
            pltpu.VMEM((every * tok, width), bf),
            pltpu.VMEM((n_dp, n_exp, 8, tok), f32),
            pltpu.VMEM((n_dp, slots, hid_r), bf),
            pltpu.VMEM((n_dp, hid_s, group), bf),
            pltpu.VMEM((n_dp, slots, hid_r), bf),
            pltpu.VMEM((n_dp, hid_s, group), bf),
            pltpu.VMEM((slots, width), bf),
            pltpu.VMEM((slots, width), bf),
            pltpu.VMEM((n_dp, n_exp, 8, tok), f32),
            pltpu.VMEM((n_dp, n_exp, 8, tok), f32),
            pltpu.VMEM((n_exp, 8, tok), f32),
            pltpu.VMEM((n_exp, 8, tok), f32),
            dma((every,)), dma((every,)),
            dma((n_exp,)), dma((n_exp,)),
            dma((n_dp,)), dma((n_dp,)),
            dma((n_dp,)), dma((n_dp,)), dma((n_dp,)), dma((n_dp,)),
            dma((n_dp,)), dma((n_dp,)), dma((n_dp,)), dma((n_dp,)),
            dma((n_dp,)), dma((n_dp,)),
            dma((n_exp,)), dma((n_exp,)),
            dma((4,)),
        ],
        compiler_params=pltpu.CompilerParams(
            collective_id=0, has_side_effects=True, vmem_limit_bytes=56 << 20
        ),
        cost_estimate=pl.CostEstimate(flops=flops, bytes_accessed=16 << 20, transcendentals=0),
    )(grad_out, meta, routed_pre[0, 0], shared_pre.T, routed_down[0], shared_down)
    return (
        out_r.reshape(routed_pre.shape),
        grad_r[None],
        out_s.T,
        grad_s,
        gate[:2].T,
    )


def by_tokens(mesh, shapes):
    n_dp, n_exp = mesh.shape["dp"], mesh.shape["expert"]
    tokens, (hidden, shared) = shapes[0][0], (shapes[4][1], shapes[6][0])
    powers = n_dp & (n_dp - 1) == 0 and n_exp & (n_exp - 1) == 0
    aligned = hidden % (128 * n_dp) == 0 and shared % (16 * n_dp * n_exp) == 0
    return powers and aligned and tokens <= hidden + shared // n_exp


def solution(mesh):
    in_specs = (
        P(("dp", "expert"), None),
        P(("dp", "expert"), None),
        P(("dp", "expert"), None),
        P("dp", "expert", None, None),
        P("expert", "dp", None),
        P("dp", "expert"),
        P(("expert", "dp"), None),
    )
    out_specs = (
        P("dp", "expert", None, None),
        P("expert", "dp", None),
        P("dp", "expert"),
        P(("expert", "dp"), None),
        P(("dp", "expert"), None),
    )

    def run(*args):
        chosen = token_body if by_tokens(mesh, [a.shape for a in args]) else body
        return jax.shard_map(
            chosen, mesh=mesh, in_specs=in_specs, out_specs=out_specs, check_vma=False
        )(*args)

    return run
```

```python
import functools

import jax
import jax.numpy as jnp
from jax import lax
from jax.experimental import pallas as pl
from jax.experimental.pallas import tpu as pltpu
from jax.sharding import PartitionSpec as P

SQRT_TWO_PI = 0.7978845608028654


def gelu_pair(inputs):
    cubic = inputs * inputs * inputs
    tangent = jnp.tanh(SQRT_TWO_PI * (inputs + 0.044715 * cubic))
    value = 0.5 * inputs * (1.0 + tangent)
    slope = 0.5 * (1.0 + tangent) + 0.5 * inputs * (1.0 - tangent * tangent) * SQRT_TWO_PI * (
        1.0 + 3.0 * 0.044715 * inputs * inputs
    )
    return (value, slope)


def slot_ranks(flat_ids, experts):
    labels = jnp.arange(experts, dtype=jnp.int32)
    onehot = (flat_ids[:, :, None] == labels[None, None, :]).astype(jnp.int32)
    before = jnp.cumsum(onehot, axis=1) - onehot
    return jnp.sum(before * onehot, axis=2)


def body(grad_out, expert_ids, gates, routed_pre, routed_down, shared_pre, shared_down):
    n_exp = lax.axis_size("expert")
    tok = grad_out.shape[0]
    width = grad_out.shape[1]
    slots = routed_pre.shape[2]
    cap = slots // n_exp
    owner = lax.axis_index("expert")
    gate_b = gates.astype(jnp.bfloat16)
    whole_down, whole_shared = (
        lax.all_gather(routed_down, "dp", axis=1, tiled=True),
        lax.all_gather(shared_down, "dp", axis=0, tiled=True),
    )
    own_rank = slot_ranks(expert_ids.reshape(1, tok * 2), n_exp).reshape(tok, 2)
    group_rows, group_gate = (
        lax.all_gather(grad_out, "expert", axis=0, tiled=True),
        lax.all_gather(gate_b, "expert", axis=0, tiled=True),
    )
    group_ids = lax.all_gather(expert_ids, "expert", axis=0, tiled=True)
    group_rank = slot_ranks(group_ids.reshape(n_exp, tok * 2), n_exp).reshape(n_exp * tok, 2)
    source = jnp.arange(n_exp * tok, dtype=jnp.int32) // tok
    target = jnp.where(group_ids == owner, source[:, None] * cap + group_rank, slots)
    recv_rows = jnp.zeros((slots + 1, width), jnp.bfloat16)
    recv_rows = recv_rows.at[target[:, 0]].set(group_rows).at[target[:, 1]].set(group_rows)[:slots]
    recv_gate = jnp.zeros((slots + 1,), jnp.bfloat16).at[target].set(group_gate)[:slots]
    value, slope = gelu_pair(routed_pre[0, 0].astype(jnp.float32))
    hidden_b = value.astype(jnp.bfloat16)
    raw = lax.dot_general(
        recv_rows, whole_down[0], (((1,), (1,)), ((), ())), preferred_element_type=jnp.float32
    )
    gate_col = recv_gate.astype(jnp.float32)[:, None]
    routed_pre_grad = (gate_col * raw * slope).astype(jnp.bfloat16).reshape(routed_pre.shape)
    slot_score = jnp.sum(value * raw, axis=1)
    scaled = (gate_col * recv_rows.astype(jnp.float32)).astype(jnp.bfloat16)
    routed_term = lax.dot_general(
        hidden_b, scaled, (((0,), (0,)), ((), ())), preferred_element_type=jnp.float32
    )
    returned = lax.all_to_all(
        slot_score.reshape(n_exp, cap), "expert", split_axis=0, concat_axis=0, tiled=True
    )
    gate_grad = returned[expert_ids, own_rank]
    svalue, sslope = gelu_pair(shared_pre.astype(jnp.float32))
    shared_b = svalue.astype(jnp.bfloat16)
    raw_shared = lax.dot_general(
        group_rows, whole_shared, (((1,), (1,)), ((), ())), preferred_element_type=jnp.float32
    )
    shared_pre_grad = (raw_shared * sslope).astype(jnp.bfloat16)
    shared_term = lax.dot_general(
        shared_b, group_rows, (((0,), (0,)), ((), ())), preferred_element_type=jnp.float32
    )
    routed_sum, shared_sum = (
        lax.psum_scatter(
            routed_term.astype(jnp.bfloat16), "dp", scatter_dimension=0, tiled=True
        ).astype(jnp.float32),
        lax.psum_scatter(
            shared_term.astype(jnp.bfloat16), "dp", scatter_dimension=0, tiled=True
        ).astype(jnp.float32),
    )
    return (
        routed_pre_grad,
        routed_sum.reshape(1, routed_sum.shape[0], width),
        shared_pre_grad,
        shared_sum,
        gate_grad,
    )


def flip(value, mask, bits):
    out = 0
    for bit in range(bits):
        has = lax.rem(value // (1 << bit), 2)
        out = out + ((1 - has) if (mask >> bit) & 1 else has) * (1 << bit)
    return out


def flip_by(value, mask, bits):
    out = 0
    for bit in range(bits):
        a, b = lax.rem(value // (1 << bit), 2), lax.rem(mask // (1 << bit), 2)
        out = out + (a + b - 2 * a * b) * (1 << bit)
    return out


def token_kernel(
    dp_bits, exp_bits, cap,
    grad, meta, pre_r, pre_s, down_r, down_s,
    out_r, out_s, grad_r, grad_s, gate_out,
    rows, metas, in_r, in_s, stage_r, stage_s, routed, scaled, gate_part, gate_recv, gate_sum, gate_last,
    ag_send, ag_recv, m1_send, m1_recv, m2_send, m2_recv,
    inr_send, inr_recv, ins_send, ins_recv, outr_send, outr_recv, outs_send, outs_recv,
    g1_send, g1_recv, g2_send, g2_recv, local,
):
    n_dp, n_exp = 1 << dp_bits, 1 << exp_bits
    d, e = lax.axis_index("dp"), lax.axis_index("expert")
    own = d * n_exp + e
    bits = dp_bits + exp_bits
    tok = grad.shape[0]
    hid_r, hid_s = down_r.shape[0], down_s.shape[0]
    group = n_exp * tok

    def dp_peer(mask):
        return {"dp": flip(d, mask, dp_bits), "expert": e}

    def exp_peer(mask):
        return {"dp": d, "expert": flip(e, mask, exp_bits)}

    def peer(bit):
        return exp_peer(1 << bit) if bit < exp_bits else dp_peer(1 << (bit - exp_bits))

    def remote(source, target, send, recv, device):
        return pltpu.make_async_remote_copy(
            src_ref=source, dst_ref=target, send_sem=send, recv_sem=recv,
            device_id=device, device_id_type=pl.DeviceIdType.MESH,
        )

    barrier = pltpu.get_barrier_semaphore()
    for mask in range(1, n_dp):
        pl.semaphore_signal(barrier, inc=1, device_id=dp_peer(mask), device_id_type=pl.DeviceIdType.MESH)
    for mask in range(1, n_exp):
        pl.semaphore_signal(barrier, inc=1, device_id=exp_peer(mask), device_id_type=pl.DeviceIdType.MESH)

    def rows_of(mask):
        at = pl.multiple_of(flip(own, mask, bits) * tok, tok)
        return rows.at[pl.ds(at, tok), :]

    rows[pl.ds(pl.multiple_of(own * tok, tok), tok), :] = grad[...]
    metas[d, e] = meta[...]
    own_r = pltpu.make_async_copy(
        pre_r.at[:, pl.ds(pl.multiple_of(d * hid_r, hid_r), hid_r)], in_r.at[0], local.at[0]
    )
    own_s = pltpu.make_async_copy(
        pre_s.at[pl.ds(pl.multiple_of(d * hid_s, hid_s), hid_s), :], in_s.at[0], local.at[1]
    )
    own_r.start()
    own_s.start()
    pl.semaphore_wait(barrier, n_dp + n_exp - 2)

    def hop(mask, bit):
        got = mask | (1 << bit)
        return remote(rows_of(mask), rows_of(mask), ag_send.at[got], ag_recv.at[got], peer(bit))

    def arrived(mask):
        return remote(rows_of(mask), rows_of(mask), ag_send.at[mask], ag_recv.at[mask], peer(0))

    order = list(range(bits))[::-1]
    meta_first = [
        remote(metas.at[d, e], metas.at[d, e], m1_send.at[mask], m1_recv.at[mask], exp_peer(mask))
        for mask in range(1, n_exp)
    ]
    for copy in meta_first:
        copy.start()
    for bit in order:
        hop(0, bit).start()

    def give(mask):
        to = flip(d, mask, dp_bits)
        remote(
            pre_r.at[:, pl.ds(pl.multiple_of(to * hid_r, hid_r), hid_r)],
            in_r.at[mask], inr_send.at[mask], inr_recv.at[mask], dp_peer(mask),
        ).start()
        remote(
            pre_s.at[pl.ds(pl.multiple_of(to * hid_s, hid_s), hid_s), :],
            in_s.at[mask], ins_send.at[mask], ins_recv.at[mask], dp_peer(mask),
        ).start()

    for mask in range(1, n_exp):
        came = metas.at[d, flip(e, mask, exp_bits)]
        remote(came, came, m1_send.at[mask], m1_recv.at[mask], exp_peer(mask)).wait_recv()
    for mask in range(1, n_dp):
        remote(metas.at[d], metas.at[d], m2_send.at[mask], m2_recv.at[mask], dp_peer(mask)).start()

    grad_r[...] = jnp.zeros_like(grad_r)
    grad_s[...] = jnp.zeros_like(grad_s)
    gate_part[...] = jnp.zeros_like(gate_part)

    held = [0]
    for place, bit in enumerate(order):
        fresh = [mask | (1 << bit) for mask in held]
        for mask in fresh:
            arrived(mask).wait_recv()
            for later in order[place + 1:]:
                hop(mask, later).start()
        held = held + fresh
        if bit == exp_bits + 1:
            for mask in range(n_dp - 2, 0, -2):
                give(mask)
        if bit == exp_bits:
            for mask in range(n_dp - 1, 0, -2):
                give(mask)
    for mask in range(1, n_dp):
        came = metas.at[flip(d, mask, dp_bits)]
        remote(came, came, m2_send.at[mask], m2_recv.at[mask], dp_peer(mask)).wait_recv()
    own_r.wait()
    own_s.wait()

    columns = pl.ds(pl.multiple_of(d * hid_r, hid_r), hid_r)
    lines = pl.ds(pl.multiple_of(d * hid_s, hid_s), hid_s)

    @pl.loop(0, n_dp)
    def _(turn):
        mask = n_dp - 1 - turn
        if dp_bits == 3:
            high, middle, low = turn // 4, lax.rem(turn // 2, 2), lax.rem(turn, 2)
            mask = 4 * (1 - high) + 2 * (1 - low) + middle
        p = flip_by(d, mask, dp_bits)
        target = {"dp": p, "expert": e}

        @pl.when(mask > 0)
        def _():
            remote(in_r.at[mask], in_r.at[mask], inr_send.at[mask], inr_recv.at[mask], target).wait_recv()
            remote(in_s.at[mask], in_s.at[mask], ins_send.at[mask], ins_recv.at[mask], target).wait_recv()

        group_rows = rows[pl.ds(pl.multiple_of(p * group, group), group), :]
        raw_s = lax.dot_general(
            down_s[...], group_rows, (((1,), (1,)), ((), ())), preferred_element_type=jnp.float32
        )
        value_s, slope_s = gelu_pair(in_s[mask].astype(jnp.float32))
        stage_s[mask] = (raw_s * slope_s).astype(jnp.bfloat16)

        gate_cols = []
        picks = []
        line = lax.broadcasted_iota(jnp.int32, (cap, tok), 0).astype(jnp.float32)
        expert = e.astype(jnp.float32)
        for s in range(n_exp):
            info = metas[p, s]
            pick0 = (info[0:1] == expert) & (info[2:3] == line)
            pick1 = (info[1:2] == expert) & (info[3:4] == line)
            gate = info[4:6].astype(jnp.bfloat16).astype(jnp.float32)
            weight = jnp.where(pick0, gate[0:1], 0.0) + jnp.where(pick1, gate[1:2], 0.0)
            chosen = (jnp.where(pick0, 1.0, 0.0) + jnp.where(pick1, 1.0, 0.0)).astype(jnp.bfloat16)
            block = lax.dot_general(
                chosen, group_rows[s * tok:(s + 1) * tok], (((1,), (0,)), ((), ())),
                preferred_element_type=jnp.float32,
            )
            gate_col = jnp.sum(weight, axis=1, keepdims=True)
            routed[s * cap:(s + 1) * cap, :] = block.astype(jnp.bfloat16)
            scaled[s * cap:(s + 1) * cap, :] = (gate_col * block).astype(jnp.bfloat16)
            gate_cols.append(gate_col)
            picks.append((pick0, pick1))
        raw = lax.dot_general(
            routed[...], down_r[...], (((1,), (1,)), ((), ())), preferred_element_type=jnp.float32
        )
        value, slope = gelu_pair(in_r[mask].astype(jnp.float32))
        stage_r[mask] = (jnp.concatenate(gate_cols, axis=0) * raw * slope).astype(jnp.bfloat16)
        score = jnp.sum(value * raw, axis=1, keepdims=True)
        for s in range(n_exp):
            part = score[s * cap:(s + 1) * cap]
            for k in range(2):
                gate_part[mask, s, k:k + 1, :] = jnp.sum(
                    jnp.where(picks[s][k], part, 0.0), axis=0, keepdims=True
                )

        @pl.when(mask > 0)
        def _():
            remote(stage_r.at[mask], out_r.at[:, columns], outr_send.at[mask], outr_recv.at[mask], target).start()
            remote(stage_s.at[mask], out_s.at[lines, :], outs_send.at[mask], outs_recv.at[mask], target).start()
            remote(gate_part.at[mask], gate_recv.at[mask], g1_send.at[mask], g1_recv.at[mask], target).start()

        grad_s[...] += lax.dot_general(
            value_s.astype(jnp.bfloat16), group_rows, (((1,), (0,)), ((), ())), preferred_element_type=jnp.float32
        )
        grad_r[...] += lax.dot_general(
            value.astype(jnp.bfloat16), scaled[...], (((0,), (0,)), ((), ())), preferred_element_type=jnp.float32
        )

    last_r = pltpu.make_async_copy(stage_r.at[0], out_r.at[:, columns], local.at[2])
    last_s = pltpu.make_async_copy(stage_s.at[0], out_s.at[lines, :], local.at[3])
    last_r.start()
    last_s.start()

    total = gate_part[0]
    for mask in range(1, n_dp):
        remote(
            gate_recv.at[mask], gate_recv.at[mask], g1_send.at[mask], g1_recv.at[mask], dp_peer(mask)
        ).wait_recv()
        total = total + gate_recv[mask]
    gate_sum[...] = total
    for mask in range(1, n_exp):
        remote(
            gate_sum.at[flip(e, mask, exp_bits)], gate_last.at[mask], g2_send.at[mask], g2_recv.at[mask], exp_peer(mask)
        ).start()
    final = gate_sum[e]
    for mask in range(1, n_exp):
        remote(
            gate_last.at[mask], gate_last.at[mask], g2_send.at[mask], g2_recv.at[mask], exp_peer(mask)
        ).wait_recv()
        final = final + gate_last[mask]
    gate_out[...] = final

    for mask in range(1, n_dp):
        origin = flip(d, mask, dp_bits)
        from_r = out_r.at[:, pl.ds(pl.multiple_of(origin * hid_r, hid_r), hid_r)]
        from_s = out_s.at[pl.ds(pl.multiple_of(origin * hid_s, hid_s), hid_s), :]
        remote(stage_r.at[mask], from_r, outr_send.at[mask], outr_recv.at[mask], dp_peer(mask)).wait()
        remote(stage_s.at[mask], from_s, outs_send.at[mask], outs_recv.at[mask], dp_peer(mask)).wait()
        remote(in_r.at[mask], in_r.at[mask], inr_send.at[mask], inr_recv.at[mask], dp_peer(mask)).wait_send()
        remote(in_s.at[mask], in_s.at[mask], ins_send.at[mask], ins_recv.at[mask], dp_peer(mask)).wait_send()
        remote(metas.at[d], metas.at[d], m2_send.at[mask], m2_recv.at[mask], dp_peer(mask)).wait_send()
        remote(
            gate_part.at[mask], gate_recv.at[mask], g1_send.at[mask], g1_recv.at[mask], dp_peer(mask)
        ).wait_send()
    for mask in range(1, n_exp):
        remote(metas.at[d, e], metas.at[d, e], m1_send.at[mask], m1_recv.at[mask], exp_peer(mask)).wait_send()
        remote(
            gate_sum.at[flip(e, mask, exp_bits)], gate_last.at[mask], g2_send.at[mask], g2_recv.at[mask], exp_peer(mask)
        ).wait_send()
    for mask in range(1, n_dp * n_exp):
        arrived(mask).wait_send()
    last_r.wait()
    last_s.wait()


def token_body(grad_out, expert_ids, gates, routed_pre, routed_down, shared_pre, shared_down):
    n_dp, n_exp = lax.axis_size("dp"), lax.axis_size("expert")
    dp_bits, exp_bits = n_dp.bit_length() - 1, n_exp.bit_length() - 1
    tok, width = grad_out.shape
    slots, hidden = routed_pre.shape[2:]
    cap = slots // n_exp
    hid_r, hid_s = routed_down.shape[1], shared_down.shape[0]
    group, shared_hidden = shared_pre.shape
    flat = expert_ids.reshape(tok * 2)
    place = jnp.arange(tok * 2, dtype=jnp.int32)
    rank = jnp.sum(
        ((flat[None, :] == flat[:, None]) & (place[None, :] < place[:, None])).astype(jnp.float32), axis=1
    ).reshape(tok, 2)
    meta = jnp.concatenate(
        [expert_ids.astype(jnp.float32).T, rank.T, gates.T, jnp.zeros((2, tok), jnp.float32)], axis=0
    )
    any_spec, vmem = pl.BlockSpec(memory_space=pl.ANY), pl.BlockSpec(memory_space=pltpu.VMEM)
    bf, f32, dma = jnp.bfloat16, jnp.float32, pltpu.SemaphoreType.DMA
    every = n_dp * n_exp
    flops = 4 * n_dp * width * (slots * hid_r + group * hid_s)
    out_r, out_s, grad_r, grad_s, gate = pl.pallas_call(
        functools.partial(token_kernel, dp_bits, exp_bits, cap),
        out_shape=[
            jax.ShapeDtypeStruct((slots, hidden), bf),
            jax.ShapeDtypeStruct((shared_hidden, group), bf),
            jax.ShapeDtypeStruct((hid_r, width), f32),
            jax.ShapeDtypeStruct((hid_s, width), f32),
            jax.ShapeDtypeStruct((8, tok), f32),
        ],
        in_specs=[vmem, vmem, any_spec, any_spec, vmem, vmem],
        out_specs=[any_spec, any_spec, vmem, vmem, vmem],
        scratch_shapes=[
            pltpu.VMEM((every * tok, width), bf),
            pltpu.VMEM((n_dp, n_exp, 8, tok), f32),
            pltpu.VMEM((n_dp, slots, hid_r), bf),
            pltpu.VMEM((n_dp, hid_s, group), bf),
            pltpu.VMEM((n_dp, slots, hid_r), bf),
            pltpu.VMEM((n_dp, hid_s, group), bf),
            pltpu.VMEM((slots, width), bf),
            pltpu.VMEM((slots, width), bf),
            pltpu.VMEM((n_dp, n_exp, 8, tok), f32),
            pltpu.VMEM((n_dp, n_exp, 8, tok), f32),
            pltpu.VMEM((n_exp, 8, tok), f32),
            pltpu.VMEM((n_exp, 8, tok), f32),
            dma((every,)), dma((every,)),
            dma((n_exp,)), dma((n_exp,)),
            dma((n_dp,)), dma((n_dp,)),
            dma((n_dp,)), dma((n_dp,)), dma((n_dp,)), dma((n_dp,)),
            dma((n_dp,)), dma((n_dp,)), dma((n_dp,)), dma((n_dp,)),
            dma((n_dp,)), dma((n_dp,)),
            dma((n_exp,)), dma((n_exp,)),
            dma((4,)),
        ],
        compiler_params=pltpu.CompilerParams(
            collective_id=0, has_side_effects=True, vmem_limit_bytes=56 << 20
        ),
        cost_estimate=pl.CostEstimate(flops=flops, bytes_accessed=16 << 20, transcendentals=0),
    )(grad_out, meta, routed_pre[0, 0], shared_pre.T, routed_down[0], shared_down)
    return (
        out_r.reshape(routed_pre.shape),
        grad_r[None],
        out_s.T,
        grad_s,
        gate[:2].T,
    )


def by_tokens(mesh, shapes):
    n_dp, n_exp = mesh.shape["dp"], mesh.shape["expert"]
    tokens, (hidden, shared) = shapes[0][0], (shapes[4][1], shapes[6][0])
    powers = n_dp & (n_dp - 1) == 0 and n_exp & (n_exp - 1) == 0
    aligned = hidden % (128 * n_dp) == 0 and shared % (16 * n_dp * n_exp) == 0
    return powers and aligned and tokens <= hidden + shared // n_exp


def solution(mesh):
    in_specs = (
        P(("dp", "expert"), None),
        P(("dp", "expert"), None),
        P(("dp", "expert"), None),
        P("dp", "expert", None, None),
        P("expert", "dp", None),
        P("dp", "expert"),
        P(("expert", "dp"), None),
    )
    out_specs = (
        P("dp", "expert", None, None),
        P("expert", "dp", None),
        P("dp", "expert"),
        P(("expert", "dp"), None),
        P(("dp", "expert"), None),
    )

    def run(*args):
        chosen = token_body if by_tokens(mesh, [a.shape for a in args]) else body
        return jax.shard_map(
            chosen, mesh=mesh, in_specs=in_specs, out_specs=out_specs, check_vma=False
        )(*args)

    return run
```

```python
import functools

import jax
import jax.numpy as jnp
from jax import lax
from jax.experimental import pallas as pl
from jax.experimental.pallas import tpu as pltpu
from jax.sharding import PartitionSpec as P

SQRT_TWO_PI = 0.7978845608028654


def gelu_pair(inputs):
    cubic = inputs * inputs * inputs
    tangent = jnp.tanh(SQRT_TWO_PI * (inputs + 0.044715 * cubic))
    value = 0.5 * inputs * (1.0 + tangent)
    slope = 0.5 * (1.0 + tangent) + 0.5 * inputs * (1.0 - tangent * tangent) * SQRT_TWO_PI * (
        1.0 + 3.0 * 0.044715 * inputs * inputs
    )
    return (value, slope)


def slot_ranks(flat_ids, experts):
    labels = jnp.arange(experts, dtype=jnp.int32)
    onehot = (flat_ids[:, :, None] == labels[None, None, :]).astype(jnp.int32)
    before = jnp.cumsum(onehot, axis=1) - onehot
    return jnp.sum(before * onehot, axis=2)


def body(grad_out, expert_ids, gates, routed_pre, routed_down, shared_pre, shared_down):
    n_exp = lax.axis_size("expert")
    tok = grad_out.shape[0]
    width = grad_out.shape[1]
    slots = routed_pre.shape[2]
    cap = slots // n_exp
    owner = lax.axis_index("expert")
    gate_b = gates.astype(jnp.bfloat16)
    whole_down, whole_shared = (
        lax.all_gather(routed_down, "dp", axis=1, tiled=True),
        lax.all_gather(shared_down, "dp", axis=0, tiled=True),
    )
    own_rank = slot_ranks(expert_ids.reshape(1, tok * 2), n_exp).reshape(tok, 2)
    group_rows, group_gate = (
        lax.all_gather(grad_out, "expert", axis=0, tiled=True),
        lax.all_gather(gate_b, "expert", axis=0, tiled=True),
    )
    group_ids = lax.all_gather(expert_ids, "expert", axis=0, tiled=True)
    group_rank = slot_ranks(group_ids.reshape(n_exp, tok * 2), n_exp).reshape(n_exp * tok, 2)
    source = jnp.arange(n_exp * tok, dtype=jnp.int32) // tok
    target = jnp.where(group_ids == owner, source[:, None] * cap + group_rank, slots)
    recv_rows = jnp.zeros((slots + 1, width), jnp.bfloat16)
    recv_rows = recv_rows.at[target[:, 0]].set(group_rows).at[target[:, 1]].set(group_rows)[:slots]
    recv_gate = jnp.zeros((slots + 1,), jnp.bfloat16).at[target].set(group_gate)[:slots]
    value, slope = gelu_pair(routed_pre[0, 0].astype(jnp.float32))
    hidden_b = value.astype(jnp.bfloat16)
    raw = lax.dot_general(
        recv_rows, whole_down[0], (((1,), (1,)), ((), ())), preferred_element_type=jnp.float32
    )
    gate_col = recv_gate.astype(jnp.float32)[:, None]
    routed_pre_grad = (gate_col * raw * slope).astype(jnp.bfloat16).reshape(routed_pre.shape)
    slot_score = jnp.sum(value * raw, axis=1)
    scaled = (gate_col * recv_rows.astype(jnp.float32)).astype(jnp.bfloat16)
    routed_term = lax.dot_general(
        hidden_b, scaled, (((0,), (0,)), ((), ())), preferred_element_type=jnp.float32
    )
    returned = lax.all_to_all(
        slot_score.reshape(n_exp, cap), "expert", split_axis=0, concat_axis=0, tiled=True
    )
    gate_grad = returned[expert_ids, own_rank]
    svalue, sslope = gelu_pair(shared_pre.astype(jnp.float32))
    shared_b = svalue.astype(jnp.bfloat16)
    raw_shared = lax.dot_general(
        group_rows, whole_shared, (((1,), (1,)), ((), ())), preferred_element_type=jnp.float32
    )
    shared_pre_grad = (raw_shared * sslope).astype(jnp.bfloat16)
    shared_term = lax.dot_general(
        shared_b, group_rows, (((0,), (0,)), ((), ())), preferred_element_type=jnp.float32
    )
    routed_sum, shared_sum = (
        lax.psum_scatter(
            routed_term.astype(jnp.bfloat16), "dp", scatter_dimension=0, tiled=True
        ).astype(jnp.float32),
        lax.psum_scatter(
            shared_term.astype(jnp.bfloat16), "dp", scatter_dimension=0, tiled=True
        ).astype(jnp.float32),
    )
    return (
        routed_pre_grad,
        routed_sum.reshape(1, routed_sum.shape[0], width),
        shared_pre_grad,
        shared_sum,
        gate_grad,
    )


def flip(value, mask, bits):
    out = 0
    for bit in range(bits):
        has = lax.rem(value // (1 << bit), 2)
        out = out + ((1 - has) if (mask >> bit) & 1 else has) * (1 << bit)
    return out


def flip_by(value, mask, bits):
    out = 0
    for bit in range(bits):
        a, b = lax.rem(value // (1 << bit), 2), lax.rem(mask // (1 << bit), 2)
        out = out + (a + b - 2 * a * b) * (1 << bit)
    return out


def token_kernel(
    dp_bits, exp_bits, cap,
    grad, meta, pre_r, pre_s, down_r, down_s,
    out_r, out_s, grad_r, grad_s, gate_out,
    rows, metas, in_r, in_s, stage_r, stage_s, routed, scaled,
    weight_r, weight_s, far_r, far_s, sent_r, sent_s, got_r, got_s,
    gate_part, gate_recv, gate_sum, gate_last,
    ag_send, ag_recv, m1_send, m1_recv, m2_send, m2_recv,
    inr_send, inr_recv, ins_send, ins_recv, outr_send, outr_recv, outs_send, outs_recv,
    g1_send, g1_recv, g2_send, g2_recv, pair_send, pair_recv, local,
):
    n_exp, low_bits = 1 << exp_bits, dp_bits - 1
    n_low = 1 << low_bits
    d, e = lax.axis_index("dp"), lax.axis_index("expert")
    low = lax.rem(d, n_low)
    base = d - low
    own = low * n_exp + e
    bits = low_bits + exp_bits
    tok = grad.shape[0]
    hid_r, hid_s = down_r.shape[0], down_s.shape[0]
    group = n_exp * tok

    def dp_peer(mask):
        return {"dp": flip(d, mask, dp_bits), "expert": e}

    def exp_peer(mask):
        return {"dp": d, "expert": flip(e, mask, exp_bits)}

    def peer(bit):
        return exp_peer(1 << bit) if bit < exp_bits else dp_peer(1 << (bit - exp_bits))

    def remote(source, target, send, recv, device):
        return pltpu.make_async_remote_copy(
            src_ref=source, dst_ref=target, send_sem=send, recv_sem=recv,
            device_id=device, device_id_type=pl.DeviceIdType.MESH,
        )

    def columns(at):
        return pl.ds(pl.multiple_of(at * hid_r, hid_r), hid_r)

    def lines(at):
        return pl.ds(pl.multiple_of(at * hid_s, hid_s), hid_s)

    def side_of(value, side):
        return flip(value, side * n_low, dp_bits)

    barrier = pltpu.get_barrier_semaphore()
    partners = [dp_peer(mask) for mask in range(1, n_low + 1)] + [exp_peer(mask) for mask in range(1, n_exp)]
    for device in partners:
        pl.semaphore_signal(barrier, inc=1, device_id=device, device_id_type=pl.DeviceIdType.MESH)

    def rows_of(mask):
        at = pl.multiple_of(flip(own, mask, bits) * tok, tok)
        return rows.at[pl.ds(at, tok), :]

    rows[pl.ds(pl.multiple_of(own * tok, tok), tok), :] = grad[...]
    metas[low, e] = meta[...]
    locals_in = []
    for side in range(2):
        at = side_of(d, side)
        locals_in.append(pltpu.make_async_copy(pre_r.at[:, columns(at)], in_r.at[side], local.at[2 * side]))
        locals_in.append(pltpu.make_async_copy(pre_s.at[lines(at), :], in_s.at[side], local.at[2 * side + 1]))
    for copy in locals_in:
        copy.start()
    pl.semaphore_wait(barrier, len(partners))

    def hop(mask, bit):
        got = mask | (1 << bit)
        return remote(rows_of(mask), rows_of(mask), ag_send.at[got], ag_recv.at[got], peer(bit))

    def arrived(mask):
        return remote(rows_of(mask), rows_of(mask), ag_send.at[mask], ag_recv.at[mask], peer(0))

    def give(mask):
        for side in (1, 0):
            at = side_of(flip(d, mask, dp_bits), side)
            slot = 2 * mask + side
            remote(
                pre_r.at[:, columns(at)], in_r.at[slot], inr_send.at[slot], inr_recv.at[slot], dp_peer(mask)
            ).start()
            remote(
                pre_s.at[lines(at), :], in_s.at[slot], ins_send.at[slot], ins_recv.at[slot], dp_peer(mask)
            ).start()

    def pair(source, target, index):
        return remote(source, target, pair_send.at[index], pair_recv.at[index], dp_peer(n_low))

    order = list(range(bits))[::-1]
    for mask in range(1, n_exp):
        remote(metas.at[low, e], metas.at[low, e], m1_send.at[mask], m1_recv.at[mask], exp_peer(mask)).start()
    for bit in order:
        hop(0, bit).start()
    weights = [pair(down_s, weight_s.at[1], 1), pair(down_r, weight_r.at[1], 0)]
    for copy in weights:
        copy.start()
    for mask in range(1, n_exp):
        came = metas.at[low, flip(e, mask, exp_bits)]
        remote(came, came, m1_send.at[mask], m1_recv.at[mask], exp_peer(mask)).wait_recv()
    for mask in range(1, n_low):
        remote(metas.at[low], metas.at[low], m2_send.at[mask], m2_recv.at[mask], dp_peer(mask)).start()

    for ref in (grad_r, grad_s, far_r, far_s, gate_part):
        ref[...] = jnp.zeros_like(ref)
    weight_r[0] = down_r[...]
    weight_s[0] = down_s[...]

    held = [0]
    for place, bit in enumerate(order):
        fresh = [mask | (1 << bit) for mask in held]
        for mask in fresh:
            arrived(mask).wait_recv()
            for later in order[place + 1:]:
                hop(mask, later).start()
        held = held + fresh
        if bit == exp_bits + 1:
            for mask in range(n_low - 2, 0, -2):
                give(mask)
        if bit == exp_bits:
            for mask in range(n_low - 1, 0, -2):
                give(mask)
    for mask in range(1, n_low):
        came = metas.at[flip(low, mask, low_bits)]
        remote(came, came, m2_send.at[mask], m2_recv.at[mask], dp_peer(mask)).wait_recv()
    for copy in locals_in:
        copy.wait()

    line = lax.broadcasted_iota(jnp.int32, (cap, tok), 0).astype(jnp.float32)
    expert = e.astype(jnp.float32)

    def picked(place, s):
        info = metas[place, s]
        pick0 = (info[0:1] == expert) & (info[2:3] == line)
        pick1 = (info[1:2] == expert) & (info[3:4] == line)
        gate = info[4:6].astype(jnp.bfloat16).astype(jnp.float32)
        weight = jnp.where(pick0, gate[0:1], 0.0) + jnp.where(pick1, gate[1:2], 0.0)
        return pick0, pick1, jnp.sum(weight, axis=1, keepdims=True)

    @pl.loop(0, n_low)
    def _(mask):
        place = flip_by(low, mask, low_bits)
        device = {"dp": base + place, "expert": e}

        @pl.when(mask > 0)
        def _():
            for side in range(2):
                slot = 2 * mask + side
                remote(in_r.at[slot], in_r.at[slot], inr_send.at[slot], inr_recv.at[slot], device).wait_recv()
                remote(in_s.at[slot], in_s.at[slot], ins_send.at[slot], ins_recv.at[slot], device).wait_recv()

        group_rows = rows[pl.ds(pl.multiple_of(place * group, group), group), :]
        for s in range(n_exp):
            pick0, pick1, gate_col = picked(place, s)
            chosen = (jnp.where(pick0, 1.0, 0.0) + jnp.where(pick1, 1.0, 0.0)).astype(jnp.bfloat16)
            block = lax.dot_general(
                chosen, group_rows[s * tok:(s + 1) * tok], (((1,), (0,)), ((), ())),
                preferred_element_type=jnp.float32,
            )
            routed[mask, s * cap:(s + 1) * cap, :] = block.astype(jnp.bfloat16)
            scaled[s * cap:(s + 1) * cap, :] = (gate_col * block).astype(jnp.bfloat16)
        for side, (sum_r, sum_s) in ((1, (far_r, far_s)), (0, (grad_r, grad_s))):
            value_s, _ = gelu_pair(in_s[2 * mask + side].astype(jnp.float32))
            sum_s[...] += lax.dot_general(
                value_s.astype(jnp.bfloat16), group_rows, (((1,), (0,)), ((), ())),
                preferred_element_type=jnp.float32,
            )
            value_r, _ = gelu_pair(in_r[2 * mask + side].astype(jnp.float32))
            sum_r[...] += lax.dot_general(
                value_r.astype(jnp.bfloat16), scaled[...], (((0,), (0,)), ((), ())),
                preferred_element_type=jnp.float32,
            )

    sent_r[...] = far_r[...].astype(jnp.bfloat16)
    sent_s[...] = far_s[...].astype(jnp.bfloat16)
    sums = [pair(sent_r, got_r, 2), pair(sent_s, got_s, 3)]
    for copy in sums:
        copy.start()

    @pl.loop(0, 2 * n_low)
    def _(turn):
        side = turn // n_low
        mask = n_low - 1 - lax.rem(turn, n_low)
        slot = 2 * mask + side
        place = flip_by(low, mask, low_bits)
        device = {"dp": base + place, "expert": e}
        at = lax.rem(d + side * n_low, 2 * n_low)

        @pl.when(turn == n_low)
        def _():
            for copy in weights:
                copy.wait_recv()

        group_rows = rows[pl.ds(pl.multiple_of(place * group, group), group), :]
        raw_s = lax.dot_general(
            weight_s[side], group_rows, (((1,), (1,)), ((), ())), preferred_element_type=jnp.float32
        )
        _, slope_s = gelu_pair(in_s[slot].astype(jnp.float32))
        stage_s[slot] = (raw_s * slope_s).astype(jnp.bfloat16)
        raw = lax.dot_general(
            routed[mask], weight_r[side], (((1,), (1,)), ((), ())), preferred_element_type=jnp.float32
        )
        value, slope = gelu_pair(in_r[slot].astype(jnp.float32))
        picks = [picked(place, s) for s in range(n_exp)]
        gate_col = jnp.concatenate([pick[2] for pick in picks], axis=0)
        stage_r[slot] = (gate_col * raw * slope).astype(jnp.bfloat16)

        @pl.when(mask > 0)
        def _():
            remote(
                stage_r.at[slot], out_r.at[:, columns(at)], outr_send.at[slot], outr_recv.at[slot], device
            ).start()
            remote(
                stage_s.at[slot], out_s.at[lines(at), :], outs_send.at[slot], outs_recv.at[slot], device
            ).start()

        score = jnp.sum(value * raw, axis=1, keepdims=True)
        for s in range(n_exp):
            part = score[s * cap:(s + 1) * cap]
            for k in range(2):
                gate_part[mask, s, k:k + 1, :] += jnp.sum(
                    jnp.where(picks[s][k], part, 0.0), axis=0, keepdims=True
                )

        @pl.when((mask > 0) & (side == 1))
        def _():
            remote(gate_part.at[mask], gate_recv.at[mask], g1_send.at[mask], g1_recv.at[mask], device).start()

    locals_out = []
    for side in range(2):
        at = side_of(d, side)
        locals_out.append(pltpu.make_async_copy(stage_r.at[side], out_r.at[:, columns(at)], local.at[4 + 2 * side]))
        locals_out.append(pltpu.make_async_copy(stage_s.at[side], out_s.at[lines(at), :], local.at[5 + 2 * side]))
    for copy in locals_out:
        copy.start()

    total = gate_part[0]
    for mask in range(1, n_low):
        remote(
            gate_recv.at[mask], gate_recv.at[mask], g1_send.at[mask], g1_recv.at[mask], dp_peer(mask)
        ).wait_recv()
        total = total + gate_recv[mask]
    gate_sum[...] = total
    for mask in range(1, n_exp):
        remote(
            gate_sum.at[flip(e, mask, exp_bits)], gate_last.at[mask], g2_send.at[mask], g2_recv.at[mask], exp_peer(mask)
        ).start()
    final = gate_sum[e]
    for mask in range(1, n_exp):
        remote(
            gate_last.at[mask], gate_last.at[mask], g2_send.at[mask], g2_recv.at[mask], exp_peer(mask)
        ).wait_recv()
        final = final + gate_last[mask]
    gate_out[...] = final

    for copy in sums:
        copy.wait()
    grad_r[...] += got_r[...].astype(jnp.float32)
    grad_s[...] += got_s[...].astype(jnp.float32)

    for mask in range(1, n_low):
        for side in range(2):
            slot = 2 * mask + side
            origin = side_of(flip(d, mask, dp_bits), side)
            remote(
                stage_r.at[slot], out_r.at[:, columns(origin)], outr_send.at[slot], outr_recv.at[slot], dp_peer(mask)
            ).wait()
            remote(
                stage_s.at[slot], out_s.at[lines(origin), :], outs_send.at[slot], outs_recv.at[slot], dp_peer(mask)
            ).wait()
            remote(in_r.at[slot], in_r.at[slot], inr_send.at[slot], inr_recv.at[slot], dp_peer(mask)).wait_send()
            remote(in_s.at[slot], in_s.at[slot], ins_send.at[slot], ins_recv.at[slot], dp_peer(mask)).wait_send()
        remote(metas.at[low], metas.at[low], m2_send.at[mask], m2_recv.at[mask], dp_peer(mask)).wait_send()
        remote(
            gate_part.at[mask], gate_recv.at[mask], g1_send.at[mask], g1_recv.at[mask], dp_peer(mask)
        ).wait_send()
    for mask in range(1, n_exp):
        remote(metas.at[low, e], metas.at[low, e], m1_send.at[mask], m1_recv.at[mask], exp_peer(mask)).wait_send()
        remote(
            gate_sum.at[flip(e, mask, exp_bits)], gate_last.at[mask], g2_send.at[mask], g2_recv.at[mask], exp_peer(mask)
        ).wait_send()
    for mask in range(1, n_low * n_exp):
        arrived(mask).wait_send()
    for copy in weights:
        copy.wait_send()
    for copy in locals_out:
        copy.wait()


def token_body(grad_out, expert_ids, gates, routed_pre, routed_down, shared_pre, shared_down):
    n_dp, n_exp = lax.axis_size("dp"), lax.axis_size("expert")
    dp_bits, exp_bits = n_dp.bit_length() - 1, n_exp.bit_length() - 1
    tok, width = grad_out.shape
    slots, hidden = routed_pre.shape[2:]
    cap = slots // n_exp
    hid_r, hid_s = routed_down.shape[1], shared_down.shape[0]
    group, shared_hidden = shared_pre.shape
    flat = expert_ids.reshape(tok * 2)
    place = jnp.arange(tok * 2, dtype=jnp.int32)
    rank = jnp.sum(
        ((flat[None, :] == flat[:, None]) & (place[None, :] < place[:, None])).astype(jnp.float32), axis=1
    ).reshape(tok, 2)
    meta = jnp.concatenate(
        [expert_ids.astype(jnp.float32).T, rank.T, gates.T, jnp.zeros((2, tok), jnp.float32)], axis=0
    )
    any_spec, vmem = pl.BlockSpec(memory_space=pl.ANY), pl.BlockSpec(memory_space=pltpu.VMEM)
    bf, f32, dma = jnp.bfloat16, jnp.float32, pltpu.SemaphoreType.DMA
    n_low = n_dp // 2
    every = n_low * n_exp
    flops = 4 * n_dp * width * (slots * hid_r + group * hid_s)
    out_r, out_s, grad_r, grad_s, gate = pl.pallas_call(
        functools.partial(token_kernel, dp_bits, exp_bits, cap),
        out_shape=[
            jax.ShapeDtypeStruct((slots, hidden), bf),
            jax.ShapeDtypeStruct((shared_hidden, group), bf),
            jax.ShapeDtypeStruct((hid_r, width), f32),
            jax.ShapeDtypeStruct((hid_s, width), f32),
            jax.ShapeDtypeStruct((8, tok), f32),
        ],
        in_specs=[vmem, vmem, any_spec, any_spec, vmem, vmem],
        out_specs=[any_spec, any_spec, vmem, vmem, vmem],
        scratch_shapes=[
            pltpu.VMEM((every * tok, width), bf),
            pltpu.VMEM((n_low, n_exp, 8, tok), f32),
            pltpu.VMEM((n_dp, slots, hid_r), bf),
            pltpu.VMEM((n_dp, hid_s, group), bf),
            pltpu.VMEM((n_dp, slots, hid_r), bf),
            pltpu.VMEM((n_dp, hid_s, group), bf),
            pltpu.VMEM((n_low, slots, width), bf),
            pltpu.VMEM((slots, width), bf),
            pltpu.VMEM((2, hid_r, width), bf),
            pltpu.VMEM((2, hid_s, width), bf),
            pltpu.VMEM((hid_r, width), f32),
            pltpu.VMEM((hid_s, width), f32),
            pltpu.VMEM((hid_r, width), bf),
            pltpu.VMEM((hid_s, width), bf),
            pltpu.VMEM((hid_r, width), bf),
            pltpu.VMEM((hid_s, width), bf),
            pltpu.VMEM((n_low, n_exp, 8, tok), f32),
            pltpu.VMEM((n_low, n_exp, 8, tok), f32),
            pltpu.VMEM((n_exp, 8, tok), f32),
            pltpu.VMEM((n_exp, 8, tok), f32),
            dma((every,)), dma((every,)),
            dma((n_exp,)), dma((n_exp,)),
            dma((n_low,)), dma((n_low,)),
            dma((n_dp,)), dma((n_dp,)), dma((n_dp,)), dma((n_dp,)),
            dma((n_dp,)), dma((n_dp,)), dma((n_dp,)), dma((n_dp,)),
            dma((n_low,)), dma((n_low,)),
            dma((n_exp,)), dma((n_exp,)),
            dma((4,)), dma((4,)),
            dma((8,)),
        ],
        compiler_params=pltpu.CompilerParams(
            collective_id=0, has_side_effects=True, vmem_limit_bytes=56 << 20
        ),
        cost_estimate=pl.CostEstimate(flops=flops, bytes_accessed=16 << 20, transcendentals=0),
    )(grad_out, meta, routed_pre[0, 0], shared_pre.T, routed_down[0], shared_down)
    return (
        out_r.reshape(routed_pre.shape),
        grad_r[None],
        out_s.T,
        grad_s,
        gate[:2].T,
    )


def by_tokens(mesh, shapes):
    n_dp, n_exp = mesh.shape["dp"], mesh.shape["expert"]
    tokens, (hidden, shared) = shapes[0][0], (shapes[4][1], shapes[6][0])
    powers = n_dp > 1 and n_dp & (n_dp - 1) == 0 and n_exp & (n_exp - 1) == 0
    aligned = hidden % (128 * n_dp) == 0 and shared % (16 * n_dp * n_exp) == 0
    return powers and aligned and tokens <= hidden + shared // n_exp


def solution(mesh):
    in_specs = (
        P(("dp", "expert"), None),
        P(("dp", "expert"), None),
        P(("dp", "expert"), None),
        P("dp", "expert", None, None),
        P("expert", "dp", None),
        P("dp", "expert"),
        P(("expert", "dp"), None),
    )
    out_specs = (
        P("dp", "expert", None, None),
        P("expert", "dp", None),
        P("dp", "expert"),
        P(("expert", "dp"), None),
        P(("dp", "expert"), None),
    )

    def run(*args):
        chosen = token_body if by_tokens(mesh, [a.shape for a in args]) else body
        return jax.shard_map(
            chosen, mesh=mesh, in_specs=in_specs, out_specs=out_specs, check_vma=False
        )(*args)

    return run
```
